256 devices in a mesh: tgt: 32 (over z, y_lo, core), blk: 8 (over x, y_hi).
Axes of the slice: x: 4, y: 4 (y_hi: 2, y_lo: 2; y = y_hi * 2 + y_lo), z: 8, core: 2. Of those that a mesh axis runs over, the one named last changes fastest.
Arguments:
- target_feats: bfloat16 [32768, 32768], P('tgt', 'blk'), may hold values from -6 to 6
- support_feats: bfloat16 [512, 32768], P('tgt', 'blk'), may hold values from -6 to 6
- coefs: bfloat16 [1000, 512], replicated, may hold values from -0.25 to 0.25
- labels: int32 [32768], P('tgt'), may hold values from 0 to 999
Outputs:
- support_grad: float32 [512, 32768], P('tgt', 'blk')
- coef_grad: float32 [1000, 512], P('blk')
The draws below stay inside these ranges and needn't reach their ends.
All inputs are finite; a program needn't handle non-finite values.
Results may differ from the reference program's by a relative error of at most 0.0031.
Values may be sent and summed in bfloat16 or wider, within the bound.
No kernel may reach another device: no remote copies, remote signals or barrier semaphores. Data moves between devices by JAX's collectives and lax.ppermute only.
A program may use at most 64 MiB of HBM per device.

```python
import math
import jax
import jax.numpy as jnp
from jax import lax

FEATURES = 32768
CLASSES = 1000
TARGETS = 32768
SUPPORT = 512


def plant(values, rng, low, top_value):
    longest = values.shape.index(max(values.shape))
    spots = []
    for shift in (0, 1):
        where = [jax.random.randint(jax.random.fold_in(rng, axis), (), 0, length) for axis, length in enumerate(values.shape)]
        where[longest] = (where[longest] + shift) % values.shape[longest]
        spots.append(tuple(where))
    return values.at[spots[0]].set(low).at[spots[1]].set(top_value)


def block_levels(own_key, extent, cuts, smallest, high):
    loudness = 1.0
    for axis_at, parts in cuts:
        draws = jax.random.uniform(jax.random.fold_in(jax.random.fold_in(own_key, 6), axis_at), (parts,), jnp.float32, smallest / len(cuts), high / len(cuts))
        loudness = loudness * jnp.repeat(jnp.exp(draws), extent[axis_at] // parts).reshape((-1,) + (1,) * (len(extent) - 1 - axis_at))
    return loudness


def scatter_about(stream_key, extent, deviation, bound, pieces=(), kind=jnp.bfloat16):
    array = deviation * jax.random.normal(stream_key, extent, jnp.float32)
    if pieces:
        array = array * block_levels(stream_key, extent, pieces, -0.22, 0.18)
    return jnp.clip(array, -bound, bound).astype(kind)


def setup_inputs(seed: int = 0) -> dict:
    seeds = jax.random.split(jax.random.key(seed), 5)
    return {
        "target_feats": scatter_about(seeds[0], (TARGETS, FEATURES), 1.0, 6.0, ((0, 32), (1, 8))),
        "support_feats": scatter_about(seeds[1], (SUPPORT, FEATURES), 1.0, 6.0, ((0, 32), (1, 8))),
        "coefs": scatter_about(seeds[2], (CLASSES, SUPPORT), SUPPORT ** -0.5, 0.25),
        "labels": plant(jax.random.randint(seeds[3], (TARGETS,), 0, CLASSES), jax.random.fold_in(seeds[3], 1), 0, CLASSES - 1).astype(jnp.int32),
    }


def reference(target_feats, support_feats, coefs, labels):
    scale = 1.0 / math.sqrt(FEATURES)
    kernel = lax.dot_general(support_feats, target_feats, (((1,), (1,)), ((), ())), preferred_element_type=jnp.float32) * scale
    kernel_low = kernel.astype(jnp.bfloat16)
    predict = jnp.dot(coefs, kernel_low, preferred_element_type=jnp.float32)
    onehot = (jnp.arange(CLASSES, dtype=jnp.int32)[:, None] == labels[None, :]).astype(jnp.float32)
    residual = predict - onehot
    residual_low = residual.astype(jnp.bfloat16)
    kernel_grad = lax.dot_general(coefs, residual_low, (((0,), (0,)), ((), ())), preferred_element_type=jnp.float32).astype(jnp.bfloat16)
    support_grad = jnp.dot(kernel_grad, target_feats, preferred_element_type=jnp.float32) * scale
    coef_grad = lax.dot_general(residual_low, kernel_low, (((1,), (1,)), ((), ())), preferred_element_type=jnp.float32) / math.sqrt(TARGETS)
    return (support_grad, coef_grad)
```

```python
import math

import jax
import jax.numpy as jnp
from jax import lax
from jax.sharding import PartitionSpec as P

FEATURES = 32768
LOW = jnp.bfloat16
FULL = jnp.float32
DEPTH, PAIR, CORES = 8, 2, 2


def tgt_move(array, dz, dy, dc):
    pairs = []
    for z in range(DEPTH):
        for y in range(PAIR):
            for c in range(CORES):
                source = (z * PAIR + y) * CORES + c
                target = ((z + dz) % DEPTH * PAIR + (y + dy) % PAIR) * CORES + (c + dc) % CORES
                pairs.append((source, target))
    return lax.ppermute(array, "tgt", pairs)


def z_xor(array, bit):
    per = PAIR * CORES
    return lax.ppermute(array, "tgt", [(i, ((i // per) ^ bit) * per + i % per) for i in range(DEPTH * per)])


def place():
    index = lax.axis_index("tgt")
    return index // (PAIR * CORES), index // CORES % PAIR, index % CORES


def gather_support(support):
    levels, offsets = [], []
    up = down = support
    ring = [([support], [0])]
    for step in range(1, DEPTH // 2 + 1):
        up = tgt_move(up, 1, 0, 0)
        if step < DEPTH // 2:
            down = tgt_move(down, -1, 0, 0)
            ring.append(([up, down], [-step, step]))
        else:
            ring.append(([up], [-step]))
    for pieces, shifts in ring:
        own = jnp.concatenate(pieces, 0) if len(pieces) > 1 else pieces[0]
        near = tgt_move(own, 0, 1, 0)
        both = jnp.concatenate([own, near], 0)
        other = tgt_move(both, 0, 0, 1)
        levels.append(jnp.concatenate([both, other], 0))
        offsets.append([(dz, dy, dc) for dc in (0, 1) for dy in (0, 1) for dz in shifts])
    return levels, offsets


def order_matrix(offsets, rows):
    z, y, c = place()
    shards = [((z + dz) % DEPTH * PAIR + (y + dy) % PAIR) * CORES + (c + dc) % CORES for dz, dy, dc in offsets]
    ids = (jnp.stack(shards)[:, None] * rows + jnp.arange(rows)[None, :]).reshape(-1)
    return (ids[:, None] == jnp.arange(ids.shape[0])[None, :]).astype(LOW)


def sum_coef(part):
    z, y, c = place()
    rows, columns = part.shape

    def halves(array, which):
        half = array.shape[1] // 2
        keep = lax.dynamic_slice_in_dim(array, which * half, half, 1)
        give = lax.dynamic_slice_in_dim(array, (1 - which) * half, half, 1)
        return keep, give

    def joined(mine, other, which):
        return jnp.where(which == 0, jnp.concatenate([mine, other], 1), jnp.concatenate([other, mine], 1))

    keep, give = halves(part, c)
    part = keep + tgt_move(give, 0, 0, 1)
    keep, give = halves(part, y)
    part = keep + tgt_move(give, 0, 1, 0)
    for bit in (1, 2, 4):
        part = part + z_xor(part, bit)
    part = joined(part, tgt_move(part, 0, 1, 0), y)
    return joined(part, tgt_move(part, 0, 0, 1), c)


def shards(target_feats, support_feats, coefs, labels):
    scale = 1.0 / math.sqrt(FEATURES)
    classes = coefs.shape[0]
    targets, features = target_feats.shape
    rows = support_feats.shape[0]
    blks = lax.axis_size("blk")
    tgts = lax.axis_size("tgt")
    blk_index = lax.axis_index("blk")
    z, y, c = place()
    half = features // 2

    give = lax.dynamic_slice_in_dim(target_feats, (1 - c) * half, half, 1)
    keep = lax.dynamic_slice_in_dim(target_feats, c * half, half, 1)
    taken = tgt_move(give, 0, 0, 1)

    levels, offsets = gather_support(support_feats)
    order = order_matrix(sum(offsets, []), rows)
    coefs_here = lax.dot_general(coefs, order, (((1,), (1,)), ((), ())), preferred_element_type=FULL).astype(LOW)

    groups = [levels[:3], levels[3:]]
    low_parts = []
    for group in groups:
        block = jnp.concatenate(group, 0)
        part = lax.dot_general(target_feats, block, (((1,), (1,)), ((), ())), preferred_element_type=FULL) * scale
        got = lax.all_to_all(part.astype(LOW), "blk", 0, 0, tiled=True)
        total = jnp.sum(got.reshape(blks, targets // blks, block.shape[0]).astype(FULL), 0)
        low_parts.append(total.astype(LOW))
    own_low = jnp.concatenate(low_parts, 1)
    spread = jnp.broadcast_to(own_low[None], (blks,) + own_low.shape).reshape(targets, -1)
    kernel_low = lax.all_to_all(spread, "blk", 0, 0, tiled=True)

    predict = lax.dot_general(kernel_low, coefs_here, (((1,), (1,)), ((), ())), preferred_element_type=FULL)
    onehot = (labels[:, None] == jnp.arange(classes, dtype=jnp.int32)[None, :]).astype(FULL)
    residual_low = (predict - onehot).astype(LOW)
    kernel_grad = lax.dot_general(coefs, residual_low, (((0,), (1,)), ((), ())), preferred_element_type=FULL).astype(LOW)
    other_grad = tgt_move(kernel_grad, 0, 0, 1)

    partial = jnp.dot(kernel_grad, keep, preferred_element_type=FULL) + jnp.dot(other_grad, taken, preferred_element_type=FULL)
    z_groups = [[zz * PAIR * CORES + r for zz in range(DEPTH)] for r in range(PAIR * CORES)]
    got = lax.all_to_all(partial.astype(LOW), "tgt", 0, 0, tiled=True, axis_index_groups=z_groups)
    chip_rows = rows * PAIR * CORES
    total = jnp.sum(got.reshape(DEPTH, chip_rows, half).astype(FULL), 0)
    total = total.reshape(PAIR, CORES * rows, half)
    mine = lax.dynamic_index_in_dim(total, y, 0, False) + tgt_move(lax.dynamic_index_in_dim(total, 1 - y, 0, False), 0, 1, 0)
    mine = mine.reshape(CORES, rows, half) * scale
    here = lax.dynamic_index_in_dim(mine, c, 0, False)
    there = tgt_move(lax.dynamic_index_in_dim(mine, 1 - c, 0, False), 0, 0, 1)
    support_grad = jnp.where(c == 0, jnp.concatenate([here, there], 1), jnp.concatenate([there, here], 1))

    class_rows = classes // blks
    own_classes = lax.dynamic_slice_in_dim(residual_low, blk_index * class_rows, class_rows, 1)
    ordered = lax.dot_general(kernel_low, order, (((1,), (0,)), ((), ())), preferred_element_type=FULL).astype(LOW)
    coef_part = lax.dot_general(own_classes, ordered, (((0,), (0,)), ((), ())), preferred_element_type=FULL)
    coef_grad = sum_coef(coef_part) / math.sqrt(targets * tgts)
    return support_grad, coef_grad


def solution(mesh):
    in_specs = (P("tgt", "blk"), P("tgt", "blk"), P(), P("tgt"))
    out_specs = (P("tgt", "blk"), P("blk", None))
    return jax.shard_map(shards, mesh=mesh, in_specs=in_specs, out_specs=out_specs, check_vma=False)
```

```python
import math

import jax
import jax.numpy as jnp
from jax import lax
from jax.experimental import pallas as pl
from jax.experimental.pallas import tpu as pltpu
from jax.sharding import PartitionSpec as P

FEATURES = 32768
LOW = jnp.bfloat16
FULL = jnp.float32
DEPTH, PAIR, CORES = 8, 2, 2
FAR = DEPTH // 2
RING = (4, 3, -3, 2, -2, 1, -1, 0)


def tgt_move(array, dz, dy, dc):
    pairs = []
    for z in range(DEPTH):
        for y in range(PAIR):
            for c in range(CORES):
                source = (z * PAIR + y) * CORES + c
                target = ((z + dz) % DEPTH * PAIR + (y + dy) % PAIR) * CORES + (c + dc) % CORES
                pairs.append((source, target))
    return lax.ppermute(array, "tgt", pairs)


def place():
    index = lax.axis_index("tgt")
    return index // (PAIR * CORES), index // CORES % PAIR, index % CORES


def together(*values):
    return lax.optimization_barrier(values)


def dot(a, b, left, right):
    return lax.dot_general(a, b, (((left,), (right,)), ((), ())), preferred_element_type=FULL)


def call(kernel, out, grid, in_specs, out_specs, flops, bytes_accessed, scratch=(), prefetch=0):
    return pl.pallas_call(
        kernel,
        out_shape=out,
        grid_spec=pltpu.PrefetchScalarGridSpec(
            num_scalar_prefetch=prefetch, grid=grid, in_specs=in_specs, out_specs=out_specs, scratch_shapes=list(scratch)
        ),
        compiler_params=pltpu.CompilerParams(dimension_semantics=("arbitrary",), vmem_limit_bytes=48 * 2**20),
        cost_estimate=pl.CostEstimate(flops=flops, bytes_accessed=bytes_accessed, transcendentals=0),
    )


def kernel_part(target_feats, pieces, scale, kind, blks):
    targets, features = target_feats.shape
    rows = sum(p.shape[0] for p in pieces)
    count = len(pieces)
    tile = 256
    block = targets // blks
    per = tile // block

    def body(*refs):
        feats, parts, out, held, sem = refs[0], refs[1 : 1 + count], refs[1 + count], refs[2 + count], refs[3 + count]

        @pl.when(pl.program_id(0) == 0)
        def _():
            copies, start = [], 0
            for i, part in enumerate(parts):
                copies.append(pltpu.make_async_copy(part, held.at[pl.ds(start, part.shape[0])], sem.at[i]))
                start += part.shape[0]
            for copy in copies:
                copy.start()
            for copy in copies:
                copy.wait()

        product = lax.dot_general(feats[...], held[...], (((1,), (1,)), ((), ())), preferred_element_type=FULL)
        out[...] = (product * scale).astype(kind).reshape(per, block, rows)

    return call(
        body,
        jax.ShapeDtypeStruct((blks, block, rows), kind),
        (targets // tile,),
        [pl.BlockSpec((tile, features), lambda i: (i, 0))] + [pl.BlockSpec(memory_space=pl.ANY)] * count,
        pl.BlockSpec((per, block, rows), lambda i: (i, 0, 0)),
        2 * targets * features * rows,
        2 * features * (targets + rows) + 4 * targets * rows,
        [pltpu.VMEM((rows, features), LOW), pltpu.SemaphoreType.DMA((count,))],
    )(target_feats, *pieces)


def take_half(target_feats, which):
    targets, features = target_feats.shape
    tile = targets // 8

    def body(which_ref, feats, out):
        out[...] = feats[...]

    return call(
        body,
        jax.ShapeDtypeStruct((targets, features // 2), LOW),
        (8,),
        [pl.BlockSpec((tile, features // 2), lambda i, w: (i, w[0]))],
        pl.BlockSpec((tile, features // 2), lambda i, w: (i, 0)),
        0,
        2 * targets * features,
        prefetch=1,
    )(which, target_feats)


def gradients(kernel_low, labels, coefs_here, coefs_ring, own_coefs, order, first_class):
    targets, supports = kernel_low.shape
    padded = coefs_here.shape[0]
    own = own_coefs.shape[0]
    tile = 256
    nt = (((1,), (1,)), ((), ()))

    def body(first_ref, low, column, row, here, ring, mine, order_ref, grad, part):
        predict = lax.dot_general(low[...], here[...], nt, preferred_element_type=FULL)
        ids = lax.broadcasted_iota(jnp.int32, (tile, padded), 1)
        residual = jnp.where(ids == column[...], predict - 1.0, predict).astype(LOW)
        grad[...] = lax.dot_general(ring[...], residual, nt, preferred_element_type=FULL).astype(LOW)
        predict = lax.dot_general(mine[...], low[...], nt, preferred_element_type=FULL)
        ids = lax.broadcasted_iota(jnp.int32, (own, tile), 0) + first_ref[0]
        residual = jnp.where(ids == row[...], predict - 1.0, predict).astype(LOW)
        ordered = jnp.dot(low[...], order_ref[...], preferred_element_type=FULL).astype(LOW)
        product = jnp.dot(residual, ordered, preferred_element_type=FULL)

        @pl.when(pl.program_id(0) == 0)
        def _():
            part[...] = product

        @pl.when(pl.program_id(0) > 0)
        def _():
            part[...] += product

    whole = lambda i, f: (0, 0)
    return call(
        body,
        (jax.ShapeDtypeStruct((supports, targets), LOW), jax.ShapeDtypeStruct((own, supports), FULL)),
        (targets // tile,),
        [
            pl.BlockSpec((tile, supports), lambda i, f: (i, 0)),
            pl.BlockSpec((tile, 1), lambda i, f: (i, 0)),
            pl.BlockSpec((1, tile), lambda i, f: (0, i)),
            pl.BlockSpec((padded, supports), whole),
            pl.BlockSpec((supports, padded), whole),
            pl.BlockSpec((own, supports), whole),
            pl.BlockSpec((supports, supports), whole),
        ],
        (pl.BlockSpec((supports, tile), lambda i, f: (0, i)), pl.BlockSpec((own, supports), whole)),
        2 * targets * supports * (2 * padded + supports),
        2 * supports * (2 * targets + 3 * padded),
        prefetch=1,
    )(first_class, kernel_low, labels[:, None], labels[None, :], coefs_here, coefs_ring, own_coefs, order)


def support_part(own_grad, other_grad, target_feats, taken, which, start, count):
    targets, features = target_feats.shape
    half = features // 2
    tile = 512
    steps = half // tile

    def body(which_ref, own, other, feats, theirs, out):
        rows = pl.ds(start, count)
        out[...] = jnp.dot(own[rows, :], feats[...], preferred_element_type=FULL) + jnp.dot(
            other[rows, :], theirs[...], preferred_element_type=FULL
        )

    whole = lambda i, w: (0, 0)
    return call(
        body,
        jax.ShapeDtypeStruct((count, half), FULL),
        (steps,),
        [
            pl.BlockSpec(own_grad.shape, whole),
            pl.BlockSpec(other_grad.shape, whole),
            pl.BlockSpec((targets, tile), lambda i, w: (0, w[0] * steps + i)),
            pl.BlockSpec((targets, tile), lambda i, w: (0, i)),
        ],
        pl.BlockSpec((count, tile), lambda i, w: (0, i)),
        4 * count * targets * half,
        4 * targets * half + 4 * count * half,
        prefetch=1,
    )(which, own_grad, other_grad, target_feats, taken)


def order_matrix(shards, rows):
    ids = (jnp.stack(shards)[:, None] * rows + jnp.arange(rows)[None, :]).reshape(-1)
    return (ids[:, None] == jnp.arange(ids.shape[0])[None, :]).astype(LOW)


def split(array, which):
    half = array.shape[1] // 2
    left, right = array[:, :half], array[:, half:]
    return jnp.where(which == 0, left, right), jnp.where(which == 0, right, left)


def join(mine, other, which):
    return jnp.where(which == 0, jnp.concatenate([mine, other], 1), jnp.concatenate([other, mine], 1))


def sums(factors, coef, rows):
    z, y, c = place()
    chip_rows = rows * PAIR * CORES
    wide = factors[3].shape[1]
    half = wide // 2

    keep, give = split(coef, c)
    coef = keep + tgt_move(give, 0, 0, 1)
    keep, give = split(coef, y)
    coef = keep + tgt_move(give, 0, 1, 0)

    partial, start = {}, 0
    for count in (3, 5):
        product = support_part(*factors, start * chip_rows, count * chip_rows)
        for i in range(count):
            partial[RING[start + i]] = product[i * chip_rows : (i + 1) * chip_rows]
        start += count

    far = partial[FAR].astype(LOW)
    up, coef_up = together(far[:, :half], coef)
    down, coef_down = together(far[:, half:], coef)
    total = coef
    for step in range(FAR, 0, -1):
        if step < FAR:
            above, below = partial[step], partial[-step]
            if step == FAR - 1:
                above = jnp.concatenate([above[:, :half] + up.astype(FULL), above[:, half:]], 1)
                below = jnp.concatenate([below[:, :half], below[:, half:] + down.astype(FULL)], 1)
            else:
                above, below = above + up.astype(FULL), below + down.astype(FULL)
            up, coef_up = together(above.astype(LOW), coef_up)
            down, coef_down = together(below.astype(LOW), coef_down)
        up, coef_up = tgt_move(up, 1, 0, 0), tgt_move(coef_up, 1, 0, 0)
        down = tgt_move(down, -1, 0, 0)
        total = total + coef_up
        if step > 1:
            coef_down = tgt_move(coef_down, -1, 0, 0)
            total = total + coef_down
    mine = (partial[0] + up.astype(FULL) + down.astype(FULL)).reshape(PAIR, CORES * rows, wide)
    give, total = together(mine[1].astype(LOW), total)
    mine = (mine[0] + tgt_move(give, 0, 1, 0).astype(FULL)).reshape(CORES, rows, wide)
    total = join(total, tgt_move(total, 0, 1, 0), y)
    here = jnp.where(c == 0, mine[0], mine[1])
    give, total = together(jnp.where(c == 0, mine[1], mine[0]), total)
    support = join(here, tgt_move(give, 0, 0, 1), c)
    return support, join(total, tgt_move(total, 0, 0, 1), c)


def shards(target_feats, support_feats, coefs, labels):
    scale = 1.0 / math.sqrt(FEATURES)
    classes = coefs.shape[0]
    targets, features = target_feats.shape
    rows = support_feats.shape[0]
    blks = lax.axis_size("blk")
    tgts = lax.axis_size("tgt")
    blk_index = lax.axis_index("blk")
    z, y, c = place()

    half = features // 2
    padded = -(-classes // 128) * 128

    pair = jnp.concatenate([support_feats, tgt_move(support_feats, 0, 1, 0)], 0)
    up = down = pair
    pieces = [(pair, 0, 0), (tgt_move(pair, 0, 0, 1), 0, 1)]

    def parts(some, kind):
        return kernel_part(target_feats, [p for p, _, _ in some], scale, kind, blks)

    def offsets(some):
        return [(dz, dy, dc) for _, dz, dc in some for dy in range(PAIR)]

    for step in range(1, FAR):
        up, down = tgt_move(up, 1, 0, 0), tgt_move(down, -1, 0, 0)
        if step == 1:
            late_c, up, down = together(c, up, down)
            give = take_half(target_feats, (1 - late_c)[None])
        if step == FAR - 1:
            near, part = pieces, parts(pieces, FULL)
            up, down, part = together(up, down, part)
            near_got = lax.all_to_all(part, "blk", 0, 0, tiled=True)
            pieces = []
        pieces += [(up, -step, 0), (down, step, 0), (tgt_move(up, 0, 0, 1), -step, 1), (tgt_move(down, 0, 0, 1), step, 1)]
    up, down = tgt_move(up[:, :half], 1, 0, 0), tgt_move(down[:, half:], -1, 0, 0)
    last = jnp.concatenate([up, down], 1)
    pieces += [(last, FAR, 0), (tgt_move(last, 0, 0, 1), FAR, 1)]
    far_part, give = together(parts(pieces, LOW), give)
    far_got = lax.all_to_all(far_part, "blk", 0, 0, tiled=True)
    taken = tgt_move(give, 0, 0, 1)

    order = order_matrix(
        [((z + dz) % DEPTH * PAIR + (y + dy) % PAIR) * CORES + (c + dc) % CORES for dz, dy, dc in offsets(near + pieces)], rows
    )
    ring_order = order_matrix(
        [((z + dz) % DEPTH * PAIR + (y + dy) % PAIR) * CORES + dc for dz in RING for dy in range(PAIR) for dc in range(CORES)], rows
    )
    class_rows = classes // blks
    first_class = blk_index * class_rows
    all_coefs = jnp.pad(coefs, ((0, padded - classes), (0, 0)))
    coefs_here = dot(all_coefs, order, 1, 1).astype(LOW)
    coefs_ring = dot(ring_order, all_coefs, 1, 1).astype(LOW)
    own_coefs = lax.dynamic_slice_in_dim(coefs_here, first_class, class_rows, 0)

    own_low = jnp.concatenate([jnp.sum(got.astype(FULL), 0).astype(LOW) for got in (near_got, far_got)], 1)
    spread = jnp.broadcast_to(own_low[None], (blks,) + own_low.shape)
    kernel_low = lax.all_to_all(spread, "blk", 0, 0, tiled=True).reshape(targets, -1)

    kernel_grad, coef_part = gradients(kernel_low, labels, coefs_here, coefs_ring, own_coefs, order, first_class[None])
    other_grad = tgt_move(kernel_grad, 0, 0, 1)
    factors = (kernel_grad, other_grad, target_feats, taken, c[None])
    support_grad, coef_grad = sums(factors, coef_part, rows)
    return support_grad * scale, coef_grad / math.sqrt(targets * tgts)


def solution(mesh):
    in_specs = (P("tgt", "blk"), P("tgt", "blk"), P(), P("tgt"))
    out_specs = (P("tgt", "blk"), P("blk", None))
    return jax.shard_map(shards, mesh=mesh, in_specs=in_specs, out_specs=out_specs, check_vma=False)
```

```python
import math

import jax
import jax.numpy as jnp
from jax import lax
from jax.experimental import pallas as pl
from jax.experimental.pallas import tpu as pltpu
from jax.sharding import PartitionSpec as P

FEATURES = 32768
LOW = jnp.bfloat16
FULL = jnp.float32
HALF = jnp.float16
TOP = 13.0
DEPTH, PAIR, CORES = 8, 2, 2
FAR = DEPTH // 2
NT = (((1,), (1,)), ((), ()))
RING = (4, 3, -3, 2, -2, 1, -1, 0)


def tgt_move(array, dz, dy, dc):
    pairs = []
    for z in range(DEPTH):
        for y in range(PAIR):
            for c in range(CORES):
                source = (z * PAIR + y) * CORES + c
                target = ((z + dz) % DEPTH * PAIR + (y + dy) % PAIR) * CORES + (c + dc) % CORES
                pairs.append((source, target))
    return lax.ppermute(array, "tgt", pairs)


def place():
    index = lax.axis_index("tgt")
    return index // (PAIR * CORES), index // CORES % PAIR, index % CORES


def together(*values):
    return lax.optimization_barrier(values)


def dot(a, b, left, right):
    return lax.dot_general(a, b, (((left,), (right,)), ((), ())), preferred_element_type=FULL)


def call(kernel, out, grid, in_specs, out_specs, flops, bytes_accessed, scratch=(), prefetch=0, vmem=48):
    return pl.pallas_call(
        kernel,
        out_shape=out,
        grid_spec=pltpu.PrefetchScalarGridSpec(
            num_scalar_prefetch=prefetch, grid=grid, in_specs=in_specs, out_specs=out_specs, scratch_shapes=list(scratch)
        ),
        compiler_params=pltpu.CompilerParams(dimension_semantics=("arbitrary",), vmem_limit_bytes=vmem * 2**20),
        cost_estimate=pl.CostEstimate(flops=flops, bytes_accessed=bytes_accessed, transcendentals=0),
    )


def kernel_part(target_feats, pieces, scale, blks):
    targets, features = target_feats.shape
    rows = sum(p.shape[0] for p in pieces)
    count = len(pieces)
    tile = 256
    steps = targets // tile
    block = targets // blks
    per = tile // block

    def body(*refs):
        feats, parts = refs[0], refs[1 : 1 + count]
        out, held, peak, sem = refs[1 + count :]
        step = pl.program_id(0)

        @pl.when(step == 0)
        def _():
            copies, start = [], 0
            for i, part in enumerate(parts):
                copies.append(pltpu.make_async_copy(part, held.at[pl.ds(start, part.shape[0])], sem.at[i]))
                start += part.shape[0]
            for copy in copies:
                copy.start()
            for copy in copies:
                copy.wait()
            peak[...] = jnp.zeros_like(peak)

        product = lax.dot_general(feats[...], held[...], NT, preferred_element_type=FULL) * scale
        for i in range(per):
            out[step * per + i, :block] = product[i * block : (i + 1) * block]
        peak[...] = jnp.maximum(peak[...], jnp.max(jnp.abs(product).reshape(tile // 8, 8, rows), axis=0))

        @pl.when(step == steps - 1)
        def _():
            top = jnp.max(jnp.max(peak[...], axis=1, keepdims=True), axis=0, keepdims=True)
            power = jnp.floor(jnp.log2(jnp.maximum(top, 1e-30)))
            factor = jnp.exp2(TOP - power)
            for i in range(blks):
                out[i, :block] = out[i, :block] * factor
                out[i, block:] = jnp.broadcast_to(power, (16, rows))

    return call(
        body,
        jax.ShapeDtypeStruct((blks, block + 16, rows), FULL),
        (steps,),
        [pl.BlockSpec((tile, features), lambda i: (i, 0))] + [pl.BlockSpec(memory_space=pltpu.HBM)] * count,
        pl.BlockSpec((blks, block + 16, rows), lambda i: (0, 0, 0)),
        2 * targets * features * rows,
        2 * features * (targets + rows) + 4 * targets * rows,
        [pltpu.VMEM((rows, features), LOW), pltpu.VMEM((8, rows), FULL), pltpu.SemaphoreType.DMA((count,))],
    )(target_feats, *pieces)


def gradients(kernel_low, labels, coefs_here, coefs_ring, own_coefs, order, first_class, core):
    targets, supports = kernel_low.shape
    padded = coefs_here.shape[0]
    own = own_coefs.shape[0]
    half = supports // 2
    tile = 256
    steps = targets // tile

    def body(scalars, low, column, row, here, ring, mine, order_ref, grad, keep, give, part):
        step = pl.program_id(0)
        predict = lax.dot_general(low[...], here[...], NT, preferred_element_type=FULL)
        ids = lax.broadcasted_iota(jnp.int32, (tile, padded), 1)
        residual = jnp.where(ids == column[...], predict - 1.0, predict).astype(LOW)
        grad[...] = lax.dot_general(ring[...], residual, NT, preferred_element_type=FULL).astype(LOW)
        predict = lax.dot_general(mine[...], low[...], NT, preferred_element_type=FULL)
        ids = lax.broadcasted_iota(jnp.int32, (own, tile), 0) + scalars[0]
        residual = jnp.where(ids == row[...], predict - 1.0, predict).astype(LOW)
        ordered = jnp.dot(low[...], order_ref[...], preferred_element_type=FULL).astype(LOW)
        product = jnp.dot(residual, ordered, preferred_element_type=FULL)

        @pl.when(step == 0)
        def _():
            part[...] = product

        @pl.when(step > 0)
        def _():
            part[...] += product

        @pl.when(step == steps - 1)
        def _():
            left, right = part[:, :half], part[:, half:]
            first = scalars[1] == 0
            keep[...] = jnp.where(first, left, right)
            give[...] = jnp.where(first, right, left)

    whole = lambda i, f: (0, 0)
    piece = jax.ShapeDtypeStruct((own, half), FULL)
    return call(
        body,
        (jax.ShapeDtypeStruct((supports, targets), LOW), piece, piece),
        (steps,),
        [
            pl.BlockSpec((tile, supports), lambda i, f: (i, 0)),
            pl.BlockSpec((tile, 1), lambda i, f: (i, 0)),
            pl.BlockSpec((1, tile), lambda i, f: (0, i)),
            pl.BlockSpec((padded, supports), whole),
            pl.BlockSpec((supports, padded), whole),
            pl.BlockSpec((own, supports), whole),
            pl.BlockSpec((supports, supports), whole),
        ],
        (pl.BlockSpec((supports, tile), lambda i, f: (0, i)),) + (pl.BlockSpec((own, half), whole),) * 2,
        2 * targets * supports * (2 * padded + supports),
        2 * supports * (2 * targets + 3 * padded),
        [pltpu.VMEM((own, supports), FULL)],
        prefetch=1,
    )(jnp.stack([first_class, core]), kernel_low, labels[:, None], labels[None, :], coefs_here, coefs_ring, own_coefs, order)


def support_part(own_grad, other_grad, target_feats, taken, coef, other_coef, which, chip_rows):
    targets, features = target_feats.shape
    supports = own_grad.shape[0]
    half = features // 2
    edge = half // 2
    tile = 512
    steps = half // tile
    classes, columns = coef.shape
    rest = classes - chip_rows
    fold = 2 * columns

    def body(which_ref, own, other, feats, theirs, coef_ref, other_ref, up, down, folded, *outs):
        step = pl.program_id(0)
        product = jnp.dot(own[...], feats[...], preferred_element_type=FULL) + jnp.dot(
            other[...], theirs[...], preferred_element_type=FULL
        )
        for i, out in enumerate(outs):
            out[...] = product[(i + 1) * chip_rows : (i + 2) * chip_rows]
        far = product[:chip_rows].astype(LOW)

        @pl.when(step < steps // 2)
        def _():
            up[:, pl.ds(pl.multiple_of(step * tile, tile), tile)] = far

        @pl.when(step >= steps // 2)
        def _():
            down[:, pl.ds(pl.multiple_of((step - steps // 2) * tile, tile), tile)] = far

        @pl.when(step == 0)
        def _():
            total = coef_ref[...] + other_ref[...]
            lower = jnp.concatenate([total[chip_rows:], jnp.zeros((chip_rows - rest, columns), FULL)], 0)
            total = jnp.concatenate([total[:chip_rows], lower], 1)
            folded[...] = total
            up[:, edge:] = total.astype(LOW)
            down[:, edge:] = total.astype(LOW)

    whole = lambda i, w: (0, 0)
    first = jax.ShapeDtypeStruct((chip_rows, edge + fold), LOW)
    later = (jax.ShapeDtypeStruct((chip_rows, half), FULL),) * (len(RING) - 1)
    up, down, folded, *parts = call(
        body,
        (first, first, jax.ShapeDtypeStruct((chip_rows, fold), FULL)) + later,
        (steps,),
        [
            pl.BlockSpec(own_grad.shape, whole),
            pl.BlockSpec(other_grad.shape, whole),
            pl.BlockSpec((targets, tile), lambda i, w: (0, w[0] * steps + i)),
            pl.BlockSpec((targets, tile), lambda i, w: (0, i)),
            pl.BlockSpec(coef.shape, whole),
            pl.BlockSpec(coef.shape, whole),
        ],
        (pl.BlockSpec((chip_rows, edge + fold), whole),) * 2
        + (pl.BlockSpec((chip_rows, fold), whole),)
        + (pl.BlockSpec((chip_rows, tile), lambda i, w: (0, i)),) * (len(RING) - 1),
        4 * supports * targets * half,
        4 * targets * half + 4 * supports * half,
        prefetch=1,
    )(which, own_grad, other_grad, target_feats, taken, coef, other_coef)
    return up, down, folded, dict(zip(RING[1:], parts))


def order_matrix(shards, rows):
    ids = (jnp.stack(shards)[:, None] * rows + jnp.arange(rows)[None, :]).reshape(-1)
    return (ids[:, None] == jnp.arange(ids.shape[0])[None, :]).astype(LOW)


def split(array, which):
    half = array.shape[1] // 2
    left, right = array[:, :half], array[:, half:]
    return jnp.where(which == 0, left, right), jnp.where(which == 0, right, left)


def join(mine, other, which):
    return jnp.where(which == 0, jnp.concatenate([mine, other], 1), jnp.concatenate([other, mine], 1))


def sums(up, down, total, part, classes, rows):
    z, y, c = place()
    wide = part[0].shape[1]
    half = wide // 2
    columns = total.shape[1] // 2
    for step in range(FAR, 0, -1):
        up, down = tgt_move(up, 1, 0, 0), tgt_move(down, -1, 0, 0)
        edge = half if step == FAR else wide
        up, coef_up = up[:, :edge], up[:, edge:]
        total = total + coef_up.astype(FULL)
        if step > 1:
            down, coef_down = down[:, :edge], down[:, edge:]
            total = total + coef_down.astype(FULL)
            above, below = part[step - 1], part[1 - step]
            if step == FAR:
                up = jnp.concatenate([above[:, :half] + up.astype(FULL), above[:, half:]], 1)
                down = jnp.concatenate([below[:, :half], below[:, half:] + down.astype(FULL)], 1)
            else:
                up, down = above + up.astype(FULL), below + down.astype(FULL)
            up = jnp.concatenate([up.astype(LOW), coef_up], 1)
            down = down.astype(LOW)
            if step > 2:
                down = jnp.concatenate([down, coef_down], 1)
    mine = (part[0] + up.astype(FULL) + down.astype(FULL)).reshape(PAIR, CORES * rows, wide)
    near_rows = CORES * rows
    beside = jnp.concatenate([total[:near_rows], total[near_rows:]], 1)
    other = tgt_move(jnp.concatenate([mine[1], beside], 1).astype(LOW), 0, 1, 0)
    mine = (mine[0] + other[:, :wide].astype(FULL)).reshape(CORES, rows, wide)
    beside = beside + other[:, wide:].astype(FULL)
    span = beside.shape[1] // 2
    total = jnp.concatenate([beside[:, :span], beside[:, span:]], 0)
    coef = jnp.concatenate([total[:, i * columns : (i + 1) * columns] for i in range(2)], 0)[:classes]
    here, give = jnp.where(c == 0, mine[0], mine[1]), jnp.where(c == 0, mine[1], mine[0])
    return join(here, tgt_move(give, 0, 0, 1), c), join(coef, tgt_move(coef, 0, 0, 1), c)


def shards(target_feats, support_feats, coefs, labels):
    scale = 1.0 / math.sqrt(FEATURES)
    classes = coefs.shape[0]
    targets, features = target_feats.shape
    rows = support_feats.shape[0]
    blks = lax.axis_size("blk")
    tgts = lax.axis_size("tgt")
    blk_index = lax.axis_index("blk")
    z, y, c = place()

    half = features // 2
    padded = -(-classes // 128) * 128

    _, give = split(target_feats, c)
    taken = tgt_move(give, 0, 0, 1)
    near = tgt_move(support_feats, 0, 1, 0)
    pair = jnp.concatenate([support_feats + 0 * give[:1, :1], near], 0)
    pieces = [(pair, 0, 0), (tgt_move(pair, 0, 0, 1), 0, 1)]

    up = down = pair
    for step in range(1, FAR):
        up, down = tgt_move(up, 1, 0, 0), tgt_move(down, -1, 0, 0)
        pieces += [(up, -step, 0), (down, step, 0), (tgt_move(up, 0, 0, 1), -step, 1), (tgt_move(down, 0, 0, 1), step, 1)]
    seen = sum(p[:1, :1] for p, dz, dc in pieces if dc == 1 and abs(dz) == 1)
    left, right = up[:, :half] + 0 * (down[:1, :1] + seen), down[:, half:] + 0 * (up[:1, :1] + seen)
    up, down = tgt_move(left, 1, 0, 0), tgt_move(right, -1, 0, 0)
    last = jnp.concatenate([up, down], 1)
    pieces += [(last, FAR, 0), (tgt_move(last, 0, 0, 1), FAR, 1)]

    order = order_matrix(
        [((z + dz) % DEPTH * PAIR + (y + dy) % PAIR) * CORES + (c + dc) % CORES for _, dz, dc in pieces for dy in range(PAIR)], rows
    )
    ring_order = order_matrix(
        [((z + dz) % DEPTH * PAIR + (y + dy) % PAIR) * CORES + dc for dz in RING for dy in range(PAIR) for dc in range(CORES)], rows
    )
    class_rows = classes // blks
    first_class = blk_index * class_rows
    all_coefs = jnp.pad(coefs, ((0, padded - classes), (0, 0)))
    coefs_here = dot(all_coefs, order, 1, 1).astype(LOW)
    coefs_ring = dot(ring_order, all_coefs, 1, 1).astype(LOW)
    own_coefs = lax.dynamic_slice_in_dim(coefs_here, first_class, class_rows, 0)

    part = kernel_part(target_feats, [p for p, _, _ in pieces], scale, blks)

    got = lax.all_to_all(part.astype(HALF), "blk", 0, 0, tiled=True).astype(FULL)
    block = targets // blks
    own_low = jnp.sum(got[:, :block] * jnp.exp2(got[:, block : block + 1] - TOP), 0).astype(LOW)
    spread = jnp.broadcast_to(own_low[None], (blks,) + own_low.shape)
    kernel_low = lax.all_to_all(spread, "blk", 0, 0, tiled=True).reshape(targets, -1)

    kernel_grad, keep, give = gradients(kernel_low, labels, coefs_here, coefs_ring, own_coefs, order, first_class, c)
    other_grad, other_coef = tgt_move(kernel_grad, 0, 0, 1), tgt_move(give, 0, 0, 1)
    up, down, total, part = support_part(
        kernel_grad, other_grad, target_feats, taken, keep, other_coef, c[None], rows * PAIR * CORES
    )
    support_grad, coef_grad = sums(up, down, total, part, class_rows, rows)
    return support_grad * scale, coef_grad / math.sqrt(targets * tgts)


def solution(mesh):
    in_specs = (P("tgt", "blk"), P("tgt", "blk"), P(), P("tgt"))
    out_specs = (P("tgt", "blk"), P("blk", None))
    return jax.shard_map(shards, mesh=mesh, in_specs=in_specs, out_specs=out_specs, check_vma=False)
```

```python
import math

import jax
import jax.numpy as jnp
from jax import lax
from jax.experimental import pallas as pl
from jax.experimental.pallas import tpu as pltpu
from jax.sharding import PartitionSpec as P

FEATURES = 32768
LOW = jnp.bfloat16
FULL = jnp.float32
HALF = jnp.float16
TOP = 13.0
SUPPORT_TILE = 512
DEPTH, PAIR, CORES = 8, 2, 2
FAR = DEPTH // 2
NT = (((1,), (1,)), ((), ()))
RING = (4, 3, -3, 2, -2, 1, -1, 0)


def tgt_move(array, dz, dy, dc):
    pairs = []
    for z in range(DEPTH):
        for y in range(PAIR):
            for c in range(CORES):
                source = (z * PAIR + y) * CORES + c
                target = ((z + dz) % DEPTH * PAIR + (y + dy) % PAIR) * CORES + (c + dc) % CORES
                pairs.append((source, target))
    return lax.ppermute(array, "tgt", pairs)


def place():
    index = lax.axis_index("tgt")
    return index // (PAIR * CORES), index // CORES % PAIR, index % CORES


def together(*values):
    return lax.optimization_barrier(values)


def dot(a, b, left, right):
    return lax.dot_general(a, b, (((left,), (right,)), ((), ())), preferred_element_type=FULL)


def call(kernel, out, grid, in_specs, out_specs, flops, bytes_accessed, scratch=(), prefetch=0, vmem=48):
    return pl.pallas_call(
        kernel,
        out_shape=out,
        grid_spec=pltpu.PrefetchScalarGridSpec(
            num_scalar_prefetch=prefetch, grid=grid, in_specs=in_specs, out_specs=out_specs, scratch_shapes=list(scratch)
        ),
        compiler_params=pltpu.CompilerParams(dimension_semantics=("arbitrary",), vmem_limit_bytes=vmem * 2**20),
        cost_estimate=pl.CostEstimate(flops=flops, bytes_accessed=bytes_accessed, transcendentals=0),
    )


def kernel_part(target_feats, pieces, scale, blks):
    targets, features = target_feats.shape
    rows = sum(p.shape[0] for p in pieces)
    count = len(pieces)
    tile = 256
    block = targets // blks
    per = tile // block

    def body(*refs):
        feats, parts = refs[0], refs[1 : 1 + count]
        out, held, sem = refs[1 + count :]

        @pl.when(pl.program_id(0) == 0)
        def _():
            copies, start = [], 0
            for i, part in enumerate(parts):
                copies.append(pltpu.make_async_copy(part, held.at[pl.ds(start, part.shape[0])], sem.at[i]))
                start += part.shape[0]
            for copy in copies:
                copy.start()
            for copy in copies:
                copy.wait()

        product = lax.dot_general(feats[...], held[...], NT, preferred_element_type=FULL) * scale
        top = jnp.max(jnp.abs(product).reshape(tile // 8, 8, rows), axis=0)
        top = jnp.max(jnp.max(top, axis=1, keepdims=True), axis=0, keepdims=True)
        power = jnp.floor(jnp.log2(jnp.maximum(top, 1e-30)))
        product = product * jnp.exp2(TOP - power)
        for i in range(per):
            out[i, :block] = product[i * block : (i + 1) * block]
            out[i, block:] = jnp.broadcast_to(power, (16, rows))

    return call(
        body,
        jax.ShapeDtypeStruct((blks, block + 16, rows), FULL),
        (targets // tile,),
        [pl.BlockSpec((tile, features), lambda i: (i, 0))] + [pl.BlockSpec(memory_space=pltpu.HBM)] * count,
        pl.BlockSpec((per, block + 16, rows), lambda i: (i, 0, 0)),
        2 * targets * features * rows,
        2 * features * (targets + rows) + 4 * targets * rows,
        [pltpu.VMEM((rows, features), LOW), pltpu.SemaphoreType.DMA((count,))],
    )(target_feats, *pieces)


def gradients(kernel_low, labels, coefs_here, coefs_ring, own_coefs, order, first_class, core):
    targets, supports = kernel_low.shape
    padded = coefs_here.shape[0]
    own = own_coefs.shape[0]
    half = supports // 2
    tile = 256
    steps = targets // tile

    def body(scalars, low, column, row, here, ring, mine, order_ref, grad, keep, give, part):
        step = pl.program_id(0)
        predict = lax.dot_general(low[...], here[...], NT, preferred_element_type=FULL)
        ids = lax.broadcasted_iota(jnp.int32, (tile, padded), 1)
        residual = jnp.where(ids == column[...], predict - 1.0, predict).astype(LOW)
        grad[...] = lax.dot_general(ring[...], residual, NT, preferred_element_type=FULL).astype(LOW)
        predict = lax.dot_general(mine[...], low[...], NT, preferred_element_type=FULL)
        ids = lax.broadcasted_iota(jnp.int32, (own, tile), 0) + scalars[0]
        residual = jnp.where(ids == row[...], predict - 1.0, predict).astype(LOW)
        ordered = jnp.dot(low[...], order_ref[...], preferred_element_type=FULL).astype(LOW)
        product = jnp.dot(residual, ordered, preferred_element_type=FULL)

        @pl.when(step == 0)
        def _():
            part[...] = product

        @pl.when(step > 0)
        def _():
            part[...] += product

        @pl.when(step == steps - 1)
        def _():
            left, right = part[:, :half], part[:, half:]
            first = scalars[1] == 0
            keep[...] = jnp.where(first, left, right)
            give[...] = jnp.where(first, right, left)

    whole = lambda i, f: (0, 0)
    piece = jax.ShapeDtypeStruct((own, half), FULL)
    return call(
        body,
        (jax.ShapeDtypeStruct((supports, targets), LOW), piece, piece),
        (steps,),
        [
            pl.BlockSpec((tile, supports), lambda i, f: (i, 0)),
            pl.BlockSpec((tile, 1), lambda i, f: (i, 0)),
            pl.BlockSpec((1, tile), lambda i, f: (0, i)),
            pl.BlockSpec((padded, supports), whole),
            pl.BlockSpec((supports, padded), whole),
            pl.BlockSpec((own, supports), whole),
            pl.BlockSpec((supports, supports), whole),
        ],
        (pl.BlockSpec((supports, tile), lambda i, f: (0, i)),) + (pl.BlockSpec((own, half), whole),) * 2,
        2 * targets * supports * (2 * padded + supports),
        2 * supports * (2 * targets + 3 * padded),
        [pltpu.VMEM((own, supports), FULL)],
        prefetch=1,
    )(jnp.stack([first_class, core]), kernel_low, labels[:, None], labels[None, :], coefs_here, coefs_ring, own_coefs, order)


def support_call(body, outs, out_specs, factors, start, count, extra, extra_specs, chip_rows):
    own_grad, other_grad, target_feats, taken, which = factors
    targets, features = target_feats.shape
    half = features // 2
    steps = half // SUPPORT_TILE
    rows = slice(start * chip_rows, (start + count) * chip_rows)

    def kernel(which_ref, own, other, feats, theirs, *refs):
        body(
            jnp.dot(own[rows, :], feats[...], preferred_element_type=FULL)
            + jnp.dot(other[rows, :], theirs[...], preferred_element_type=FULL),
            *refs,
        )

    return call(
        kernel,
        outs,
        (steps,),
        [
            pl.BlockSpec(own_grad.shape, lambda i, w: (0, 0)),
            pl.BlockSpec(other_grad.shape, lambda i, w: (0, 0)),
            pl.BlockSpec((targets, SUPPORT_TILE), lambda i, w: (0, w[0] * steps + i)),
            pl.BlockSpec((targets, SUPPORT_TILE), lambda i, w: (0, i)),
        ]
        + extra_specs,
        out_specs,
        4 * count * chip_rows * targets * half,
        4 * targets * half + 4 * count * chip_rows * half,
        prefetch=1,
    )(which, own_grad, other_grad, target_feats, taken, *extra)


def support_first(factors, coef, other_coef, chip_rows):
    half = factors[3].shape[1]
    edge = half // 2
    steps = half // SUPPORT_TILE
    classes, columns = coef.shape
    rest = classes - chip_rows
    fold = 2 * columns

    def body(product, coef_ref, other_ref, up, down, folded, above, below):
        step = pl.program_id(0)
        above[...] = product[chip_rows : 2 * chip_rows]
        below[...] = product[2 * chip_rows :]
        far = product[:chip_rows].astype(LOW)

        @pl.when(step < steps // 2)
        def _():
            up[:, pl.ds(pl.multiple_of(step * SUPPORT_TILE, SUPPORT_TILE), SUPPORT_TILE)] = far

        @pl.when(step >= steps // 2)
        def _():
            down[:, pl.ds(pl.multiple_of((step - steps // 2) * SUPPORT_TILE, SUPPORT_TILE), SUPPORT_TILE)] = far

        @pl.when(step == 0)
        def _():
            total = coef_ref[...] + other_ref[...]
            lower = jnp.concatenate([total[chip_rows:], jnp.zeros((chip_rows - rest, columns), FULL)], 0)
            total = jnp.concatenate([total[:chip_rows], lower], 1)
            folded[...] = total
            up[:, edge:] = total.astype(LOW)
            down[:, edge:] = total.astype(LOW)

    whole = lambda i, w: (0, 0)
    first = jax.ShapeDtypeStruct((chip_rows, edge + fold), LOW)
    return support_call(
        body,
        (first, first, jax.ShapeDtypeStruct((chip_rows, fold), FULL)) + (jax.ShapeDtypeStruct((chip_rows, half), FULL),) * 2,
        (pl.BlockSpec((chip_rows, edge + fold), whole),) * 2
        + (pl.BlockSpec((chip_rows, fold), whole),)
        + (pl.BlockSpec((chip_rows, SUPPORT_TILE), lambda i, w: (0, i)),) * 2,
        factors,
        0,
        3,
        [coef, other_coef],
        [pl.BlockSpec(coef.shape, whole)] * 2,
        chip_rows,
    )


def support_rest(factors, chip_rows, earlier):
    half = factors[3].shape[1]
    count = len(RING) - 3

    def body(product, *refs):
        for i, out in enumerate(refs[len(earlier) :]):
            out[...] = product[i * chip_rows : (i + 1) * chip_rows]

    return support_call(
        body,
        (jax.ShapeDtypeStruct((chip_rows, half), FULL),) * count,
        (pl.BlockSpec((chip_rows, SUPPORT_TILE), lambda i, w: (0, i)),) * count,
        factors,
        3,
        count,
        list(earlier),
        [pl.BlockSpec(memory_space=pl.ANY)] * len(earlier),
        chip_rows,
    )


def order_matrix(shards, rows):
    ids = (jnp.stack(shards)[:, None] * rows + jnp.arange(rows)[None, :]).reshape(-1)
    return (ids[:, None] == jnp.arange(ids.shape[0])[None, :]).astype(LOW)


def split(array, which):
    half = array.shape[1] // 2
    left, right = array[:, :half], array[:, half:]
    return jnp.where(which == 0, left, right), jnp.where(which == 0, right, left)


def join(mine, other, which):
    return jnp.where(which == 0, jnp.concatenate([mine, other], 1), jnp.concatenate([other, mine], 1))


def sums(factors, coef, other_coef, rows):
    z, y, c = place()
    chip_rows = rows * PAIR * CORES
    classes = coef.shape[0]
    up, down, total, above, below = support_first(factors, coef, other_coef, chip_rows)
    part = {FAR - 1: above, 1 - FAR: below}
    wide = above.shape[1]
    half = wide // 2
    columns = total.shape[1] // 2
    for step in range(FAR, 0, -1):
        if step == FAR - 1:
            part.update(zip(RING[3:], support_rest(factors, chip_rows, (up, down))))
        up, down = tgt_move(up, 1, 0, 0), tgt_move(down, -1, 0, 0)
        edge = half if step == FAR else wide
        up, coef_up = up[:, :edge], up[:, edge:]
        total = total + coef_up.astype(FULL)
        if step > 1:
            down, coef_down = down[:, :edge], down[:, edge:]
            total = total + coef_down.astype(FULL)
            above, below = part[step - 1], part[1 - step]
            if step == FAR:
                up = jnp.concatenate([above[:, :half] + up.astype(FULL), above[:, half:]], 1)
                down = jnp.concatenate([below[:, :half], below[:, half:] + down.astype(FULL)], 1)
            else:
                up, down = above + up.astype(FULL), below + down.astype(FULL)
            up = jnp.concatenate([up.astype(LOW), coef_up], 1)
            down = down.astype(LOW)
            if step > 2:
                down = jnp.concatenate([down, coef_down], 1)
    mine = (part[0] + up.astype(FULL) + down.astype(FULL)).reshape(PAIR, CORES * rows, wide)
    near_rows = CORES * rows
    beside = jnp.concatenate([total[:near_rows], total[near_rows:]], 1)
    other = tgt_move(jnp.concatenate([mine[1], beside], 1).astype(LOW), 0, 1, 0)
    mine = (mine[0] + other[:, :wide].astype(FULL)).reshape(CORES, rows, wide)
    beside = beside + other[:, wide:].astype(FULL)
    span = beside.shape[1] // 2
    total = jnp.concatenate([beside[:, :span], beside[:, span:]], 0)
    coef = jnp.concatenate([total[:, i * columns : (i + 1) * columns] for i in range(2)], 0)[:classes]
    here, give = jnp.where(c == 0, mine[0], mine[1]), jnp.where(c == 0, mine[1], mine[0])
    return join(here, tgt_move(give, 0, 0, 1), c), join(coef, tgt_move(coef, 0, 0, 1), c)


def shards(target_feats, support_feats, coefs, labels):
    scale = 1.0 / math.sqrt(FEATURES)
    classes = coefs.shape[0]
    targets, features = target_feats.shape
    rows = support_feats.shape[0]
    blks = lax.axis_size("blk")
    tgts = lax.axis_size("tgt")
    blk_index = lax.axis_index("blk")
    z, y, c = place()

    half = features // 2
    padded = -(-classes // 128) * 128

    _, give = split(target_feats, c)
    taken = tgt_move(give, 0, 0, 1)
    near = tgt_move(support_feats, 0, 1, 0)
    mine = jnp.concatenate([support_feats[:, :half] + 0 * give[:rows], support_feats[:, half:]], 1)
    pair = jnp.concatenate([mine, near], 0)
    pieces = [(pair, 0, 0), (tgt_move(pair, 0, 0, 1), 0, 1)]

    up = down = pair
    later = []
    for step in range(1, FAR):
        up, down = tgt_move(up, 1, 0, 0), tgt_move(down, -1, 0, 0)
        here = [(up, -step, 0), (down, step, 0)]
        there = [(tgt_move(up, 0, 0, 1), -step, 1), (tgt_move(down, 0, 0, 1), step, 1)]
        if step < FAR - 2:
            pieces += here + there
        elif step == FAR - 2:
            pieces += here
            near_part = kernel_part(target_feats, [p for p, _, _ in pieces], scale, blks)
            later += there
        else:
            later += here + there
    seen = jnp.tile(near_part[0, : up.shape[0]].astype(LOW), (1, half // near_part.shape[2]))
    left, right = up[:, :half] + 0 * (down[:, half:] + seen), down[:, half:] + 0 * (up[:, :half] + seen)
    up, down = tgt_move(left, 1, 0, 0), tgt_move(right, -1, 0, 0)
    last = jnp.concatenate([up, down], 1)
    later += [(last, FAR, 0), (tgt_move(last, 0, 0, 1), FAR, 1)]
    far_part = kernel_part(target_feats, [p for p, _, _ in later], scale, blks)
    pieces += later

    order = order_matrix(
        [((z + dz) % DEPTH * PAIR + (y + dy) % PAIR) * CORES + (c + dc) % CORES for _, dz, dc in pieces for dy in range(PAIR)], rows
    )
    ring_order = order_matrix(
        [((z + dz) % DEPTH * PAIR + (y + dy) % PAIR) * CORES + dc for dz in RING for dy in range(PAIR) for dc in range(CORES)], rows
    )
    class_rows = classes // blks
    first_class = blk_index * class_rows
    all_coefs = jnp.pad(coefs, ((0, padded - classes), (0, 0)))
    coefs_here = dot(all_coefs, order, 1, 1).astype(LOW)
    coefs_ring = dot(ring_order, all_coefs, 1, 1).astype(LOW)
    own_coefs = lax.dynamic_slice_in_dim(coefs_here, first_class, class_rows, 0)

    part = jnp.concatenate([near_part.astype(HALF), far_part.astype(HALF)], 1)
    got = lax.all_to_all(part, "blk", 0, 0, tiled=True).astype(FULL)
    block = targets // blks
    own_low = []
    for i in range(2):
        rest = got[:, i * (block + 16) :]
        own_low.append(jnp.sum(rest[:, :block] * jnp.exp2(rest[:, block : block + 1] - TOP), 0).astype(LOW))
    own_low = jnp.concatenate(own_low, 1)
    spread = jnp.broadcast_to(own_low[None], (blks,) + own_low.shape)
    kernel_low = lax.all_to_all(spread, "blk", 0, 0, tiled=True).reshape(targets, -1)

    kernel_grad, keep, give = gradients(kernel_low, labels, coefs_here, coefs_ring, own_coefs, order, first_class, c)
    other_grad, other_coef = tgt_move(kernel_grad, 0, 0, 1), tgt_move(give, 0, 0, 1)
    factors = (kernel_grad, other_grad, target_feats, taken, c[None])
    support_grad, coef_grad = sums(factors, keep, other_coef, rows)
    return support_grad * scale, coef_grad / math.sqrt(targets * tgts)


def solution(mesh):
    in_specs = (P("tgt", "blk"), P("tgt", "blk"), P(), P("tgt"))
    out_specs = (P("tgt", "blk"), P("blk", None))
    return jax.shard_map(shards, mesh=mesh, in_specs=in_specs, out_specs=out_specs, check_vma=False)
```

```python
import math

import jax
import jax.numpy as jnp
from jax import lax
from jax.experimental import pallas as pl
from jax.experimental.pallas import tpu as pltpu
from jax.sharding import PartitionSpec as P

FEATURES = 32768
LOW = jnp.bfloat16
FULL = jnp.float32
HALF = jnp.float16
TOP = 13.0
SUPPORT_TILE = 512
DEPTH, PAIR, CORES = 8, 2, 2
FAR = DEPTH // 2
NT = (((1,), (1,)), ((), ()))
RING = (4, 3, -3, 2, -2, 1, -1, 0)


def tgt_move(array, dz, dy, dc):
    pairs = []
    for z in range(DEPTH):
        for y in range(PAIR):
            for c in range(CORES):
                source = (z * PAIR + y) * CORES + c
                target = ((z + dz) % DEPTH * PAIR + (y + dy) % PAIR) * CORES + (c + dc) % CORES
                pairs.append((source, target))
    return lax.ppermute(array, "tgt", pairs)


def place():
    index = lax.axis_index("tgt")
    return index // (PAIR * CORES), index // CORES % PAIR, index % CORES


def together(*values):
    return lax.optimization_barrier(values)


def dot(a, b, left, right):
    return lax.dot_general(a, b, (((left,), (right,)), ((), ())), preferred_element_type=FULL)


def call(kernel, out, grid, in_specs, out_specs, flops, bytes_accessed, scratch=(), prefetch=0, vmem=48):
    return pl.pallas_call(
        kernel,
        out_shape=out,
        grid_spec=pltpu.PrefetchScalarGridSpec(
            num_scalar_prefetch=prefetch, grid=grid, in_specs=in_specs, out_specs=out_specs, scratch_shapes=list(scratch)
        ),
        compiler_params=pltpu.CompilerParams(dimension_semantics=("arbitrary",), vmem_limit_bytes=vmem * 2**20),
        cost_estimate=pl.CostEstimate(flops=flops, bytes_accessed=bytes_accessed, transcendentals=0),
    )


def kernel_part(target_feats, pieces, scale, blks):
    targets, features = target_feats.shape
    rows = sum(p.shape[0] for p in pieces)
    count = len(pieces)
    depth = features // 4
    steps = features // depth
    block = targets // blks

    def body(*refs):
        feats, parts = refs[0], refs[1 : 1 + count]
        out, total = refs[1 + count :]
        step = pl.program_id(0)
        held = jnp.concatenate([part[...] for part in parts], 0)
        product = lax.dot_general(feats[...], held, NT, preferred_element_type=FULL)

        @pl.when(step == 0)
        def _():
            total[...] = product

        @pl.when(step > 0)
        def _():
            total[...] += product

        @pl.when(step == steps - 1)
        def _():
            top = jnp.max(jnp.abs(total[...]).reshape(targets // 8, 8, rows), axis=0)
            top = jnp.max(jnp.max(top, axis=1, keepdims=True), axis=0, keepdims=True) * scale
            power = jnp.floor(jnp.log2(jnp.maximum(top, 1e-30)))
            factor = jnp.exp2(TOP - power) * scale
            for i in range(blks):
                out[i, :block] = total[i * block : (i + 1) * block] * factor
                out[i, block:] = jnp.broadcast_to(power, (16, rows))

    return call(
        body,
        jax.ShapeDtypeStruct((blks, block + 16, rows), FULL),
        (steps,),
        [pl.BlockSpec((targets, depth), lambda i: (0, i))]
        + [pl.BlockSpec((p.shape[0], depth), lambda i: (0, i)) for p in pieces],
        pl.BlockSpec((blks, block + 16, rows), lambda i: (0, 0, 0)),
        2 * targets * features * rows,
        2 * features * (targets + rows) + 4 * targets * rows,
        [pltpu.VMEM((targets, rows), FULL)],
    )(target_feats, *pieces)


def gradients(kernel_low, labels, coefs_here, coefs_ring, own_coefs, order, first_class, core):
    targets, supports = kernel_low.shape
    padded = coefs_here.shape[0]
    own = own_coefs.shape[0]
    half = supports // 2
    tile = 256
    steps = targets // tile

    def body(scalars, low, column, row, here, ring, mine, order_ref, grad, keep, give, part):
        step = pl.program_id(0)
        predict = lax.dot_general(low[...], here[...], NT, preferred_element_type=FULL)
        ids = lax.broadcasted_iota(jnp.int32, (tile, padded), 1)
        residual = jnp.where(ids == column[...], predict - 1.0, predict).astype(LOW)
        grad[...] = lax.dot_general(ring[...], residual, NT, preferred_element_type=FULL).astype(LOW)
        predict = lax.dot_general(mine[...], low[...], NT, preferred_element_type=FULL)
        ids = lax.broadcasted_iota(jnp.int32, (own, tile), 0) + scalars[0]
        residual = jnp.where(ids == row[...], predict - 1.0, predict).astype(LOW)
        ordered = jnp.dot(low[...], order_ref[...], preferred_element_type=FULL).astype(LOW)
        product = jnp.dot(residual, ordered, preferred_element_type=FULL)

        @pl.when(step == 0)
        def _():
            part[...] = product

        @pl.when(step > 0)
        def _():
            part[...] += product

        @pl.when(step == steps - 1)
        def _():
            left, right = part[:, :half], part[:, half:]
            first = scalars[1] == 0
            keep[...] = jnp.where(first, left, right)
            give[...] = jnp.where(first, right, left)

    whole = lambda i, f: (0, 0)
    piece = jax.ShapeDtypeStruct((own, half), FULL)
    return call(
        body,
        (jax.ShapeDtypeStruct((supports, targets), LOW), piece, piece),
        (steps,),
        [
            pl.BlockSpec((tile, supports), lambda i, f: (i, 0)),
            pl.BlockSpec((tile, 1), lambda i, f: (i, 0)),
            pl.BlockSpec((1, tile), lambda i, f: (0, i)),
            pl.BlockSpec((padded, supports), whole),
            pl.BlockSpec((supports, padded), whole),
            pl.BlockSpec((own, supports), whole),
            pl.BlockSpec((supports, supports), whole),
        ],
        (pl.BlockSpec((supports, tile), lambda i, f: (0, i)),) + (pl.BlockSpec((own, half), whole),) * 2,
        2 * targets * supports * (2 * padded + supports),
        2 * supports * (2 * targets + 3 * padded),
        [pltpu.VMEM((own, supports), FULL)],
        prefetch=1,
    )(jnp.stack([first_class, core]), kernel_low, labels[:, None], labels[None, :], coefs_here, coefs_ring, own_coefs, order)


def support_call(body, outs, factors, start, count, extra, extra_specs, chip_rows):
    own_grad, other_grad, target_feats, taken, which = factors
    targets, features = target_feats.shape
    half = features // 2
    steps = half // SUPPORT_TILE
    rows = count * chip_rows

    def kernel(which_ref, own, other, feats, theirs, *refs):
        grads, tiles, grad_sem, tile_sem = refs[-4:]
        copies = [
            pltpu.make_async_copy(grad.at[pl.ds(start * chip_rows, rows)], grads.at[i], grad_sem.at[i])
            for i, grad in enumerate((own, other))
        ]
        first = which_ref[0] * half
        loads = []
        for j in range(steps):
            here = pl.ds(pl.multiple_of(first + j * SUPPORT_TILE, SUPPORT_TILE), SUPPORT_TILE)
            there = pl.ds(j * SUPPORT_TILE, SUPPORT_TILE)
            loads.append(
                [
                    pltpu.make_async_copy(feats.at[:, here], tiles.at[j, 0], tile_sem.at[j, 0]),
                    pltpu.make_async_copy(theirs.at[:, there], tiles.at[j, 1], tile_sem.at[j, 1]),
                ]
            )
        for copy in copies + sum(loads, []):
            copy.start()
        for copy in copies:
            copy.wait()
        for j in range(steps):
            for load in loads[j]:
                load.wait()
            product = jnp.dot(grads[0], tiles[j, 0], preferred_element_type=FULL)
            body(j, product + jnp.dot(grads[1], tiles[j, 1], preferred_element_type=FULL), *refs[:-4])

    whole = [pl.BlockSpec(o.shape, lambda i, w: (0, 0)) for o in outs]
    return call(
        kernel,
        outs,
        (1,),
        [pl.BlockSpec(memory_space=pltpu.HBM)] * 4 + extra_specs,
        tuple(whole),
        4 * rows * targets * half,
        4 * targets * half + 4 * rows * half,
        [
            pltpu.VMEM((2, rows, targets), LOW),
            pltpu.VMEM((steps, 2, targets, SUPPORT_TILE), LOW),
            pltpu.SemaphoreType.DMA((2,)),
            pltpu.SemaphoreType.DMA((steps, 2)),
        ],
        prefetch=1,
    )(which, own_grad, other_grad, target_feats, taken, *extra)


def support_first(factors, coef, other_coef, chip_rows):
    half = factors[3].shape[1]
    edge = half // 2
    classes, columns = coef.shape
    rest = classes - chip_rows
    fold = 2 * columns

    def body(j, product, coef_ref, other_ref, up, down, folded, above, below):
        here = slice(j * SUPPORT_TILE, (j + 1) * SUPPORT_TILE)
        above[:, here] = product[chip_rows : 2 * chip_rows]
        below[:, here] = product[2 * chip_rows :]
        far = product[:chip_rows].astype(LOW)
        if here.stop <= edge:
            up[:, here] = far
        else:
            down[:, here.start - edge : here.stop - edge] = far
        if j == 0:
            total = coef_ref[...] + other_ref[...]
            lower = jnp.concatenate([total[chip_rows:], jnp.zeros((chip_rows - rest, columns), FULL)], 0)
            total = jnp.concatenate([total[:chip_rows], lower], 1)
            folded[...] = total
            up[:, edge:] = total.astype(LOW)
            down[:, edge:] = total.astype(LOW)

    first = jax.ShapeDtypeStruct((chip_rows, edge + fold), LOW)
    block = jax.ShapeDtypeStruct((chip_rows, half), FULL)
    outs = (first, first, jax.ShapeDtypeStruct((chip_rows, fold), FULL), block, block)
    extra_specs = [pl.BlockSpec(coef.shape, lambda i, w: (0, 0))] * 2
    return support_call(body, outs, factors, 0, 3, [coef, other_coef], extra_specs, chip_rows)


def support_rest(factors, chip_rows, earlier):
    half = factors[3].shape[1]
    count = len(RING) - 3

    def body(j, product, *refs):
        for i, out in enumerate(refs[len(earlier) :]):
            out[:, j * SUPPORT_TILE : (j + 1) * SUPPORT_TILE] = product[i * chip_rows : (i + 1) * chip_rows]

    outs = (jax.ShapeDtypeStruct((chip_rows, half), FULL),) * count
    extra_specs = [pl.BlockSpec(memory_space=pl.ANY)] * len(earlier)
    return support_call(body, outs, factors, 3, count, list(earlier), extra_specs, chip_rows)


def order_matrix(shards, rows):
    ids = (jnp.stack(shards)[:, None] * rows + jnp.arange(rows)[None, :]).reshape(-1)
    return (ids[:, None] == jnp.arange(ids.shape[0])[None, :]).astype(LOW)


def split(array, which):
    half = array.shape[1] // 2
    left, right = array[:, :half], array[:, half:]
    return jnp.where(which == 0, left, right), jnp.where(which == 0, right, left)


def join(mine, other, which):
    return jnp.where(which == 0, jnp.concatenate([mine, other], 1), jnp.concatenate([other, mine], 1))


def sums(factors, coef, other_coef, rows):
    z, y, c = place()
    chip_rows = rows * PAIR * CORES
    classes = coef.shape[0]
    up, down, total, above, below = support_first(factors, coef, other_coef, chip_rows)
    part = {FAR - 1: above, 1 - FAR: below}
    wide = above.shape[1]
    half = wide // 2
    columns = total.shape[1] // 2
    for step in range(FAR, 0, -1):
        if step == FAR - 1:
            part.update(zip(RING[3:], support_rest(factors, chip_rows, (up, down))))
        up, down = tgt_move(up, 1, 0, 0), tgt_move(down, -1, 0, 0)
        edge = half if step == FAR else wide
        up, coef_up = up[:, :edge], up[:, edge:]
        total = total + coef_up.astype(FULL)
        if step > 1:
            down, coef_down = down[:, :edge], down[:, edge:]
            total = total + coef_down.astype(FULL)
            above, below = part[step - 1], part[1 - step]
            if step == FAR:
                up = jnp.concatenate([above[:, :half] + up.astype(FULL), above[:, half:]], 1)
                down = jnp.concatenate([below[:, :half], below[:, half:] + down.astype(FULL)], 1)
            else:
                up, down = above + up.astype(FULL), below + down.astype(FULL)
            up = jnp.concatenate([up.astype(LOW), coef_up], 1)
            down = down.astype(LOW)
            if step > 2:
                down = jnp.concatenate([down, coef_down], 1)
    mine = (part[0] + up.astype(FULL) + down.astype(FULL)).reshape(PAIR, CORES * rows, wide)
    near_rows = CORES * rows
    beside = jnp.concatenate([total[:near_rows], total[near_rows:]], 1)
    other = tgt_move(jnp.concatenate([mine[1], beside], 1).astype(LOW), 0, 1, 0)
    mine = (mine[0] + other[:, :wide].astype(FULL)).reshape(CORES, rows, wide)
    beside = beside + other[:, wide:].astype(FULL)
    span = beside.shape[1] // 2
    total = jnp.concatenate([beside[:, :span], beside[:, span:]], 0)
    coef = jnp.concatenate([total[:, i * columns : (i + 1) * columns] for i in range(2)], 0)[:classes]
    here, give = jnp.where(c == 0, mine[0], mine[1]), jnp.where(c == 0, mine[1], mine[0])
    return join(here, tgt_move(give, 0, 0, 1), c), join(coef, tgt_move(coef, 0, 0, 1), c)


def shards(target_feats, support_feats, coefs, labels):
    scale = 1.0 / math.sqrt(FEATURES)
    classes = coefs.shape[0]
    targets, features = target_feats.shape
    rows = support_feats.shape[0]
    blks = lax.axis_size("blk")
    tgts = lax.axis_size("tgt")
    blk_index = lax.axis_index("blk")
    z, y, c = place()

    half = features // 2
    padded = -(-classes // 128) * 128

    _, give = split(target_feats, c)
    taken = tgt_move(give, 0, 0, 1)
    near = tgt_move(support_feats, 0, 1, 0)
    mine = jnp.concatenate([support_feats[:, :half] + 0 * give[:rows], support_feats[:, half:]], 1)
    pair = jnp.concatenate([mine, near], 0)
    pieces = [(pair, 0, 0), (tgt_move(pair, 0, 0, 1), 0, 1)]

    up = down = pair
    later = []
    for step in range(1, FAR):
        up, down = tgt_move(up, 1, 0, 0), tgt_move(down, -1, 0, 0)
        here = [(up, -step, 0), (down, step, 0)]
        there = [(tgt_move(up, 0, 0, 1), -step, 1), (tgt_move(down, 0, 0, 1), step, 1)]
        if step < FAR - 2:
            pieces += here + there
        elif step == FAR - 2:
            pieces += here
            near_part = kernel_part(target_feats, [p for p, _, _ in pieces], scale, blks)
            later += there
        else:
            later += here + there
    seen = jnp.tile(near_part[0, : up.shape[0]].astype(LOW), (1, half // near_part.shape[2]))
    left, right = up[:, :half] + 0 * (down[:, half:] + seen), down[:, half:] + 0 * (up[:, :half] + seen)
    up, down = tgt_move(left, 1, 0, 0), tgt_move(right, -1, 0, 0)
    last = jnp.concatenate([up, down], 1)
    later += [(last, FAR, 0), (tgt_move(last, 0, 0, 1), FAR, 1)]
    far_part = kernel_part(target_feats, [p for p, _, _ in later], scale, blks)
    pieces += later

    order = order_matrix(
        [((z + dz) % DEPTH * PAIR + (y + dy) % PAIR) * CORES + (c + dc) % CORES for _, dz, dc in pieces for dy in range(PAIR)], rows
    )
    ring_order = order_matrix(
        [((z + dz) % DEPTH * PAIR + (y + dy) % PAIR) * CORES + dc for dz in RING for dy in range(PAIR) for dc in range(CORES)], rows
    )
    class_rows = classes // blks
    first_class = blk_index * class_rows
    all_coefs = jnp.pad(coefs, ((0, padded - classes), (0, 0)))
    coefs_here = dot(all_coefs, order, 1, 1).astype(LOW)
    coefs_ring = dot(ring_order, all_coefs, 1, 1).astype(LOW)
    own_coefs = lax.dynamic_slice_in_dim(coefs_here, first_class, class_rows, 0)

    part = jnp.concatenate([near_part.astype(HALF), far_part.astype(HALF)], 1)
    got = lax.all_to_all(part, "blk", 0, 0, tiled=True).astype(FULL)
    block = targets // blks
    own_low = []
    for i in range(2):
        rest = got[:, i * (block + 16) :]
        own_low.append(jnp.sum(rest[:, :block] * jnp.exp2(rest[:, block : block + 1] - TOP), 0).astype(LOW))
    own_low = jnp.concatenate(own_low, 1)
    spread = jnp.broadcast_to(own_low[None], (blks,) + own_low.shape)
    kernel_low = lax.all_to_all(spread, "blk", 0, 0, tiled=True).reshape(targets, -1)

    kernel_grad, keep, give = gradients(kernel_low, labels, coefs_here, coefs_ring, own_coefs, order, first_class, c)
    other_grad, other_coef = tgt_move(kernel_grad, 0, 0, 1), tgt_move(give, 0, 0, 1)
    factors = (kernel_grad, other_grad, target_feats, taken, c[None])
    support_grad, coef_grad = sums(factors, keep, other_coef, rows)
    return support_grad * scale, coef_grad / math.sqrt(targets * tgts)


def solution(mesh):
    in_specs = (P("tgt", "blk"), P("tgt", "blk"), P(), P("tgt"))
    out_specs = (P("tgt", "blk"), P("blk", None))
    return jax.shard_map(shards, mesh=mesh, in_specs=in_specs, out_specs=out_specs, check_vma=False)
```

```python
import math

import jax
import jax.numpy as jnp
from jax import lax
from jax.experimental import pallas as pl
from jax.experimental.pallas import tpu as pltpu
from jax.sharding import PartitionSpec as P

FEATURES = 32768
LOW = jnp.bfloat16
FULL = jnp.float32
HALF = jnp.float16
TOP = 13.0
SUPPORT_TILE = 512
DEPTH, PAIR, CORES = 8, 2, 2
FAR = DEPTH // 2
NT = (((1,), (1,)), ((), ()))
RING = (4, 3, -3, 2, -2, 1, -1, 0)


def tgt_move(array, dz, dy, dc):
    pairs = []
    for z in range(DEPTH):
        for y in range(PAIR):
            for c in range(CORES):
                source = (z * PAIR + y) * CORES + c
                target = ((z + dz) % DEPTH * PAIR + (y + dy) % PAIR) * CORES + (c + dc) % CORES
                pairs.append((source, target))
    return lax.ppermute(array, "tgt", pairs)


def place():
    index = lax.axis_index("tgt")
    return index // (PAIR * CORES), index // CORES % PAIR, index % CORES


def together(*values):
    return lax.optimization_barrier(values)


def dot(a, b, left, right):
    return lax.dot_general(a, b, (((left,), (right,)), ((), ())), preferred_element_type=FULL)


def call(kernel, out, grid, in_specs, out_specs, flops, bytes_accessed, scratch=(), prefetch=0, vmem=48):
    return pl.pallas_call(
        kernel,
        out_shape=out,
        grid_spec=pltpu.PrefetchScalarGridSpec(
            num_scalar_prefetch=prefetch, grid=grid, in_specs=in_specs, out_specs=out_specs, scratch_shapes=list(scratch)
        ),
        compiler_params=pltpu.CompilerParams(dimension_semantics=("arbitrary",), vmem_limit_bytes=vmem * 2**20),
        cost_estimate=pl.CostEstimate(flops=flops, bytes_accessed=bytes_accessed, transcendentals=0),
    )


def kernel_part(target_feats, pieces, scale, blks):
    targets, features = target_feats.shape
    rows = sum(p.shape[0] for p in pieces)
    count = len(pieces)
    depth = features // 4
    steps = features // depth
    block = targets // blks

    def body(*refs):
        feats, parts = refs[0], refs[1 : 1 + count]
        out, total = refs[1 + count :]
        step = pl.program_id(0)
        held = jnp.concatenate([part[...] for part in parts], 0)
        product = lax.dot_general(feats[...], held, NT, preferred_element_type=FULL)

        @pl.when(step == 0)
        def _():
            total[...] = product

        @pl.when(step > 0)
        def _():
            total[...] += product

        @pl.when(step == steps - 1)
        def _():
            top = jnp.max(jnp.abs(total[...]).reshape(targets // 8, 8, rows), axis=0)
            top = jnp.max(jnp.max(top, axis=1, keepdims=True), axis=0, keepdims=True) * scale
            power = jnp.floor(jnp.log2(jnp.maximum(top, 1e-30)))
            factor = jnp.exp2(TOP - power) * scale
            for i in range(blks):
                out[i, :block] = total[i * block : (i + 1) * block] * factor
                out[i, block:] = jnp.broadcast_to(power, (16, rows))

    return call(
        body,
        jax.ShapeDtypeStruct((blks, block + 16, rows), FULL),
        (steps,),
        [pl.BlockSpec((targets, depth), lambda i: (0, i))]
        + [pl.BlockSpec((p.shape[0], depth), lambda i: (0, i)) for p in pieces],
        pl.BlockSpec((blks, block + 16, rows), lambda i: (0, 0, 0)),
        2 * targets * features * rows,
        2 * features * (targets + rows) + 4 * targets * rows,
        [pltpu.VMEM((targets, rows), FULL)],
    )(target_feats, *pieces)


def gradients(kernel_low, labels, coefs_here, coefs_ring, earlier):
    targets, supports = kernel_low.shape
    padded = coefs_here.shape[0]
    tile = 256
    steps = targets // tile

    def body(low_ref, column, here, ring, earlier_ref, grad, low, sem):
        step = pl.program_id(0)
        loads = [
            pltpu.make_async_copy(low_ref.at[pl.ds(j * tile, tile)], low.at[pl.ds(j * tile, tile)], sem.at[j])
            for j in range(steps)
        ]

        @pl.when(step == 0)
        def _():
            for load in loads:
                load.start()

        for j in range(steps):

            @pl.when(step == j)
            def _():
                loads[j].wait()

        some = low[pl.ds(pl.multiple_of(step * tile, tile), tile), :]
        predict = lax.dot_general(some, here[...], NT, preferred_element_type=FULL)
        ids = lax.broadcasted_iota(jnp.int32, (tile, padded), 1)
        residual = jnp.where(ids == column[...], predict - 1.0, predict).astype(LOW)
        grad[...] = lax.dot_general(ring[...], residual, NT, preferred_element_type=FULL).astype(LOW)

    whole = lambda i: (0, 0)
    return call(
        body,
        jax.ShapeDtypeStruct((supports, targets), LOW),
        (steps,),
        [
            pl.BlockSpec(memory_space=pltpu.HBM),
            pl.BlockSpec((tile, 1), lambda i: (i, 0)),
            pl.BlockSpec((padded, supports), whole),
            pl.BlockSpec((supports, padded), whole),
            pl.BlockSpec(memory_space=pl.ANY),
        ],
        pl.BlockSpec((supports, tile), lambda i: (0, i)),
        4 * targets * supports * padded,
        4 * supports * (targets + padded),
        [pltpu.VMEM((targets, supports), LOW), pltpu.SemaphoreType.DMA((steps,))],
    )(kernel_low, labels[:, None], coefs_here, coefs_ring, earlier)


def coef_part(kernel_low, labels, own_coefs, order, first_class, core, earlier):
    targets, supports = kernel_low.shape
    own = own_coefs.shape[0]
    half = supports // 2

    def body(scalars, low_ref, row, mine, order_ref, earlier_ref, keep, give, low, sem):
        load = pltpu.make_async_copy(low_ref, low, sem)
        load.start()
        load.wait()
        predict = lax.dot_general(mine[...], low[...], NT, preferred_element_type=FULL)
        ids = lax.broadcasted_iota(jnp.int32, (own, targets), 0) + scalars[0]
        residual = jnp.where(ids == row[...], predict - 1.0, predict).astype(LOW)
        ordered = jnp.dot(low[...], order_ref[...], preferred_element_type=FULL).astype(LOW)
        part = jnp.dot(residual, ordered, preferred_element_type=FULL)
        left, right = part[:, :half], part[:, half:]
        first = scalars[1] == 0
        keep[...] = jnp.where(first, left, right)
        give[...] = jnp.where(first, right, left)

    whole = lambda i, f: (0, 0)
    piece = jax.ShapeDtypeStruct((own, half), FULL)
    return call(
        body,
        (piece, piece),
        (1,),
        [
            pl.BlockSpec(memory_space=pltpu.HBM),
            pl.BlockSpec((1, targets), whole),
            pl.BlockSpec((own, supports), whole),
            pl.BlockSpec((supports, supports), whole),
            pl.BlockSpec(memory_space=pl.ANY),
        ],
        (pl.BlockSpec((own, half), whole),) * 2,
        2 * targets * supports * (supports + 2 * own),
        4 * supports * targets,
        [pltpu.VMEM((targets, supports), LOW), pltpu.SemaphoreType.DMA],
        prefetch=1,
    )(jnp.stack([first_class, core]), kernel_low, labels[None, :], own_coefs, order, earlier)


def support_call(body, outs, factors, start, count, extra, extra_specs, chip_rows):
    own_grad, other_grad, target_feats, taken, which = factors
    targets, features = target_feats.shape
    half = features // 2
    steps = half // SUPPORT_TILE
    rows = count * chip_rows

    def kernel(which_ref, own, other, feats, theirs, *refs):
        grads, tiles, grad_sem, tile_sem = refs[-4:]
        copies = [
            pltpu.make_async_copy(grad.at[pl.ds(start * chip_rows, rows)], grads.at[i], grad_sem.at[i])
            for i, grad in enumerate((own, other))
        ]
        first = which_ref[0] * half
        loads = []
        for j in range(steps):
            here = pl.ds(pl.multiple_of(first + j * SUPPORT_TILE, SUPPORT_TILE), SUPPORT_TILE)
            there = pl.ds(j * SUPPORT_TILE, SUPPORT_TILE)
            loads.append(
                [
                    pltpu.make_async_copy(feats.at[:, here], tiles.at[j, 0], tile_sem.at[j, 0]),
                    pltpu.make_async_copy(theirs.at[:, there], tiles.at[j, 1], tile_sem.at[j, 1]),
                ]
            )
        for copy in copies + sum(loads, []):
            copy.start()
        for copy in copies:
            copy.wait()
        for j in range(steps):
            for load in loads[j]:
                load.wait()
            product = jnp.dot(grads[0], tiles[j, 0], preferred_element_type=FULL)
            body(j, product + jnp.dot(grads[1], tiles[j, 1], preferred_element_type=FULL), *refs[:-4])

    whole = [pl.BlockSpec(o.shape, lambda i, w: (0, 0)) for o in outs]
    return call(
        kernel,
        outs,
        (1,),
        [pl.BlockSpec(memory_space=pltpu.HBM)] * 4 + extra_specs,
        tuple(whole),
        4 * rows * targets * half,
        4 * targets * half + 4 * rows * half,
        [
            pltpu.VMEM((2, rows, targets), LOW),
            pltpu.VMEM((steps, 2, targets, SUPPORT_TILE), LOW),
            pltpu.SemaphoreType.DMA((2,)),
            pltpu.SemaphoreType.DMA((steps, 2)),
        ],
        prefetch=1,
    )(which, own_grad, other_grad, target_feats, taken, *extra)


def support_first(factors, chip_rows, earlier):
    half = factors[3].shape[1]
    edge = half // 2

    def body(j, product, earlier_ref, up, down, above, below):
        here = slice(j * SUPPORT_TILE, (j + 1) * SUPPORT_TILE)
        above[:, here] = product[chip_rows : 2 * chip_rows]
        below[:, here] = product[2 * chip_rows :]
        far = product[:chip_rows].astype(LOW)
        if here.stop <= edge:
            up[:, here] = far
        else:
            down[:, here.start - edge : here.stop - edge] = far

    first = jax.ShapeDtypeStruct((chip_rows, edge), LOW)
    block = jax.ShapeDtypeStruct((chip_rows, half), FULL)
    outs = (first, first, block, block)
    return support_call(body, outs, factors, 0, 3, [earlier], [pl.BlockSpec(memory_space=pl.ANY)], chip_rows)


def support_rest(factors, chip_rows, earlier):
    half = factors[3].shape[1]
    count = len(RING) - 3

    def body(j, product, *refs):
        for i, out in enumerate(refs[len(earlier) :]):
            out[:, j * SUPPORT_TILE : (j + 1) * SUPPORT_TILE] = product[i * chip_rows : (i + 1) * chip_rows]

    outs = (jax.ShapeDtypeStruct((chip_rows, half), FULL),) * count
    extra_specs = [pl.BlockSpec(memory_space=pl.ANY)] * len(earlier)
    return support_call(body, outs, factors, 3, count, list(earlier), extra_specs, chip_rows)


def order_matrix(shards, rows):
    ids = (jnp.stack(shards)[:, None] * rows + jnp.arange(rows)[None, :]).reshape(-1)
    return (ids[:, None] == jnp.arange(ids.shape[0])[None, :]).astype(LOW)


def split(array, which):
    half = array.shape[1] // 2
    left, right = array[:, :half], array[:, half:]
    return jnp.where(which == 0, left, right), jnp.where(which == 0, right, left)


def join(mine, other, which):
    return jnp.where(which == 0, jnp.concatenate([mine, other], 1), jnp.concatenate([other, mine], 1))


def sums(factors, keep, give, rows):
    z, y, c = place()
    chip_rows = rows * PAIR * CORES
    classes, columns = keep.shape
    up, down, above, below = support_first(factors, chip_rows, give)
    total = jnp.pad(keep + tgt_move(give, 0, 0, 1), ((0, 2 * chip_rows - classes), (0, 0)))
    total = jnp.concatenate([total[:chip_rows], total[chip_rows:]], 1)
    up, down = jnp.concatenate([up, total.astype(LOW)], 1), jnp.concatenate([down, total.astype(LOW)], 1)
    part = {FAR - 1: above, 1 - FAR: below}
    wide = above.shape[1]
    half = wide // 2
    for step in range(FAR, 0, -1):
        if step == FAR - 1:
            part.update(zip(RING[3:], support_rest(factors, chip_rows, (up, down))))
        up, down = tgt_move(up, 1, 0, 0), tgt_move(down, -1, 0, 0)
        edge = half if step == FAR else wide
        up, coef_up = up[:, :edge], up[:, edge:]
        total = total + coef_up.astype(FULL)
        if step > 1:
            down, coef_down = down[:, :edge], down[:, edge:]
            total = total + coef_down.astype(FULL)
            above, below = part[step - 1], part[1 - step]
            if step == FAR:
                up = jnp.concatenate([above[:, :half] + up.astype(FULL), above[:, half:]], 1)
                down = jnp.concatenate([below[:, :half], below[:, half:] + down.astype(FULL)], 1)
            else:
                up, down = above + up.astype(FULL), below + down.astype(FULL)
            up = jnp.concatenate([up.astype(LOW), coef_up], 1)
            down = down.astype(LOW)
            if step > 2:
                down = jnp.concatenate([down, coef_down], 1)
    mine = (part[0] + up.astype(FULL) + down.astype(FULL)).reshape(PAIR, CORES * rows, wide)
    near_rows = CORES * rows
    beside = jnp.concatenate([total[:near_rows], total[near_rows:]], 1)
    other = tgt_move(jnp.concatenate([mine[1], beside], 1).astype(LOW), 0, 1, 0)
    mine = (mine[0] + other[:, :wide].astype(FULL)).reshape(CORES, rows, wide)
    beside = beside + other[:, wide:].astype(FULL)
    span = beside.shape[1] // 2
    total = jnp.concatenate([beside[:, :span], beside[:, span:]], 0)
    coef = jnp.concatenate([total[:, i * columns : (i + 1) * columns] for i in range(2)], 0)[:classes]
    here, give = jnp.where(c == 0, mine[0], mine[1]), jnp.where(c == 0, mine[1], mine[0])
    return join(here, tgt_move(give, 0, 0, 1), c), join(coef, tgt_move(coef, 0, 0, 1), c)


def shards(target_feats, support_feats, coefs, labels):
    scale = 1.0 / math.sqrt(FEATURES)
    classes = coefs.shape[0]
    targets, features = target_feats.shape
    rows = support_feats.shape[0]
    blks = lax.axis_size("blk")
    tgts = lax.axis_size("tgt")
    blk_index = lax.axis_index("blk")
    z, y, c = place()

    half = features // 2
    padded = -(-classes // 128) * 128

    _, give = split(target_feats, c)
    taken = tgt_move(give, 0, 0, 1)
    near = tgt_move(support_feats, 0, 1, 0)
    mine = jnp.concatenate([support_feats[:, :half] + 0 * give[:rows], support_feats[:, half:]], 1)
    pair = jnp.concatenate([mine, near], 0)
    pieces = [(pair, 0, 0), (tgt_move(pair, 0, 0, 1), 0, 1)]

    up = down = pair
    later = []
    for step in range(1, FAR):
        up, down = tgt_move(up, 1, 0, 0), tgt_move(down, -1, 0, 0)
        here = [(up, -step, 0), (down, step, 0)]
        there = [(tgt_move(up, 0, 0, 1), -step, 1), (tgt_move(down, 0, 0, 1), step, 1)]
        if step < FAR - 2:
            pieces += here + there
        elif step == FAR - 2:
            pieces += here
            near_part = kernel_part(target_feats, [p for p, _, _ in pieces], scale, blks)
            later += there
        else:
            later += here + there
    seen = jnp.tile(near_part[0, : up.shape[0]].astype(LOW), (1, half // near_part.shape[2]))
    left, right = up[:, :half] + 0 * (down[:, half:] + seen), down[:, half:] + 0 * (up[:, :half] + seen)
    up, down = tgt_move(left, 1, 0, 0), tgt_move(right, -1, 0, 0)
    last = jnp.concatenate([up, down], 1)
    later += [(last, FAR, 0), (tgt_move(last, 0, 0, 1), FAR, 1)]
    far_part = kernel_part(target_feats, [p for p, _, _ in later], scale, blks)
    pieces += later

    order = order_matrix(
        [((z + dz) % DEPTH * PAIR + (y + dy) % PAIR) * CORES + (c + dc) % CORES for _, dz, dc in pieces for dy in range(PAIR)], rows
    )
    ring_order = order_matrix(
        [((z + dz) % DEPTH * PAIR + (y + dy) % PAIR) * CORES + dc for dz in RING for dy in range(PAIR) for dc in range(CORES)], rows
    )
    class_rows = classes // blks
    first_class = blk_index * class_rows
    all_coefs = jnp.pad(coefs, ((0, padded - classes), (0, 0)))
    coefs_here = dot(all_coefs, order, 1, 1).astype(LOW)
    coefs_ring = dot(ring_order, all_coefs, 1, 1).astype(LOW)
    own_coefs = lax.dynamic_slice_in_dim(coefs_here, first_class, class_rows, 0)

    part = jnp.concatenate([near_part.astype(HALF), far_part.astype(HALF)], 1)
    got = lax.all_to_all(part, "blk", 0, 0, tiled=True).astype(FULL)
    block = targets // blks
    own_low = []
    for i in range(2):
        rest = got[:, i * (block + 16) :]
        own_low.append(jnp.sum(rest[:, :block] * jnp.exp2(rest[:, block : block + 1] - TOP), 0).astype(LOW))
    own_low = jnp.concatenate(own_low, 1)
    spread = jnp.broadcast_to(own_low[None], (blks,) + own_low.shape)
    kernel_low = lax.all_to_all(spread, "blk", 0, 0, tiled=True).reshape(targets, -1)

    kernel_grad = gradients(kernel_low, labels, coefs_here, coefs_ring, own_coefs)
    other_grad = tgt_move(kernel_grad, 0, 0, 1)
    keep, give = coef_part(kernel_low, labels, own_coefs, order, first_class, c, kernel_grad)
    factors = (kernel_grad, other_grad, target_feats, taken, c[None])
    support_grad, coef_grad = sums(factors, keep, give, rows)
    return support_grad * scale, coef_grad / math.sqrt(targets * tgts)


def solution(mesh):
    in_specs = (P("tgt", "blk"), P("tgt", "blk"), P(), P("tgt"))
    out_specs = (P("tgt", "blk"), P("blk", None))
    return jax.shard_map(shards, mesh=mesh, in_specs=in_specs, out_specs=out_specs, check_vma=False)
```
